256 devices in a mesh: chan: 32 (over y, z_hi, core), band: 8 (over x, z_lo).
Axes of the slice: x: 4, y: 4, z: 8 (z_hi: 4, z_lo: 2; z = z_hi * 2 + z_lo), core: 2. Of those that a mesh axis runs over, the one named last changes fastest.
Arguments:
- strain: bfloat16 [8192, 4, 4096], P('chan', None, 'band'), may hold values from -6 to 6
- band_start: int32 [8], replicated, may hold values from 4 to 818
Outputs:
- coherency: bfloat16 [8, 2, 8192, 8192], P('band', None, 'chan')
The draws below stay inside these ranges and needn't reach their ends.
All inputs are finite; a program needn't handle non-finite values.
Results may differ from the reference program's by a relative error of at most 0.0056.
Values may be sent and summed in bfloat16 or wider, within the bound.
No kernel may reach another device: no remote copies, remote signals or barrier semaphores. Data moves between devices by JAX's collectives and lax.ppermute only.
A program may use at most 64 MiB of HBM per device.

```python
import math
import jax
import jax.numpy as jnp
from jax import lax

WINDOW_SAMPLES = 4096
K = 32
WINDOWS = 4
FIBRE_CHANNELS = 8192
BANDS = 8


def place_ends(drawn, key, smallest, high):
    index_at = [jax.random.randint(jax.random.fold_in(key, axis), (), 0, length) for axis, length in enumerate(drawn.shape)]
    main_axis = drawn.shape.index(max(drawn.shape))
    beside = index_at[:main_axis] + [(index_at[main_axis] + 1) % drawn.shape[main_axis]] + index_at[main_axis + 1:]
    return drawn.at[tuple(index_at)].set(smallest).at[tuple(beside)].set(high)


def levels(rng, dims, shards, low, high):
    gain = 1.0
    for position, shards_of in shards:
        heights = jax.random.uniform(jax.random.fold_in(jax.random.fold_in(rng, 6), position), (shards_of,), jnp.float32, low / len(shards), high / len(shards))
        gain = gain * jnp.repeat(jnp.exp(heights), dims[position] // shards_of).reshape((-1,) + (1,) * (len(dims) - 1 - position))
    return gain


def noise(own_key, extent, deviation, bound, split=(), held_as=jnp.bfloat16):
    array = jax.random.normal(own_key, extent, jnp.float32) * deviation
    if len(split) > 0:
        array = levels(own_key, extent, split, -0.22, 0.18) * array
    return jnp.clip(array, min=-bound, max=bound).astype(held_as)


def setup_inputs(seed: int = 0) -> dict:
    key_list = jax.random.split(jax.random.key(seed), 3)
    strain = noise(key_list[0], (FIBRE_CHANNELS, WINDOWS, WINDOW_SAMPLES), 1.0, 6.0, ((0, 32), (2, 8)))
    band_start = place_ends(jax.random.randint(key_list[1], (BANDS,), 4, WINDOW_SAMPLES // 5), jax.random.fold_in(key_list[1], 1), 4, (WINDOW_SAMPLES // 5) - 1).astype(jnp.int32)
    return dict(strain=strain, band_start=band_start)


def build_fourier_table(first_bin):
    positions = jnp.arange(WINDOW_SAMPLES, dtype=jnp.int32)
    freqs = first_bin + jnp.arange(K, dtype=jnp.int32)
    phase_angles = positions[:, None] * freqs[None, :] % WINDOW_SAMPLES
    angles = phase_angles.astype(jnp.float32) * (2.0 * math.pi / WINDOW_SAMPLES)
    taper = 0.5 - 0.5 * jnp.cos(positions.astype(jnp.float32) * (2.0 * math.pi / WINDOW_SAMPLES))
    cosine = taper[:, None] * jnp.cos(angles)
    sine = -taper[:, None] * jnp.sin(angles)
    return jnp.concatenate([cosine, sine], axis=1).astype(jnp.bfloat16)

def one_band(strain, first_bin):
    table = build_fourier_table(first_bin)
    flat = strain.reshape(FIBRE_CHANNELS * WINDOWS, WINDOW_SAMPLES)
    spectrum = jnp.dot(flat, table, preferred_element_type=jnp.float32)
    power = lax.optimization_barrier(jnp.mean(spectrum * spectrum, axis=1, keepdims=True))
    whitened = (spectrum * lax.rsqrt(power + 1e-06)).astype(jnp.bfloat16)
    panel = whitened.reshape(FIBRE_CHANNELS, WINDOWS, 2, K).transpose(0, 2, 1, 3).reshape(FIBRE_CHANNELS, 2 * WINDOWS * K)
    half_feat = WINDOWS * K
    rotated = jnp.concatenate([-panel[:, half_feat:], panel[:, :half_feat]], axis=1)
    scale = 1.0 / (2.0 * K)
    real_out = (jnp.dot(panel, panel.T, preferred_element_type=jnp.float32) * scale).astype(jnp.bfloat16)
    imag_out = (jnp.dot(panel, rotated.T, preferred_element_type=jnp.float32) * scale).astype(jnp.bfloat16)
    return jnp.stack([real_out, imag_out])

def reference(strain, band_start):
    return lax.map(lambda first_bin: one_band(strain, first_bin), band_start)
```

```python
import functools
import math

import jax
import jax.numpy as jnp
from jax import lax
from jax.experimental import pallas as pl
from jax.experimental.pallas import tpu as pltpu
from jax.sharding import Mesh, PartitionSpec as P

N = 4096
K = 32
F = 2 * K
BASE = 64
VMEM = 48 * 1024 * 1024

CHAN = ("y", "zh", "core")
BAND = ("x", "zl")


def table_kernel(start_ref, out_ref, cos_coarse, sin_coarse):
    cols = out_ref.shape[1]
    fine_n = N // BASE
    lane = lax.broadcasted_iota(jnp.int32, (BASE, cols), 1)
    row = lax.broadcasted_iota(jnp.int32, (BASE, cols), 0)
    freq = lane % K
    for b in range(cols // F):
        freq = freq + jnp.where(lane // F == b, start_ref[b], 0)
    quarter = (lane // K) % 2 * (N // 4)
    step = 2.0 * math.pi / N
    coarse = ((freq * row) % (N // BASE) * BASE).astype(jnp.float32) * step
    fine = ((freq * row + quarter) % N).astype(jnp.float32) * step
    cos_coarse[...] = jnp.cos(coarse)
    sin_coarse[...] = jnp.sin(coarse)
    cos_fine, sin_fine = jnp.cos(fine), jnp.sin(fine)
    small = row[:, :128].astype(jnp.float32)
    taper_cos, taper_sin = jnp.cos(small * step), jnp.sin(small * step)
    for c in range(fine_n):
        angle = 2.0 * math.pi * BASE * c / N
        taper = 0.5 - 0.5 * (math.cos(angle) * taper_cos - math.sin(angle) * taper_sin)
        for k in range(cols // 128):
            at = slice(k * 128, k * 128 + 128)
            value = cos_coarse[c : c + 1, at] * cos_fine[:, at] - sin_coarse[c : c + 1, at] * sin_fine[:, at]
            out_ref[c * BASE : c * BASE + BASE, at] = (taper * value).astype(out_ref.dtype)


def make_table(band_start):
    cols = band_start.shape[0] * F
    return pl.pallas_call(
        table_kernel,
        out_shape=jax.ShapeDtypeStruct((N, cols), jnp.bfloat16),
        in_specs=[pl.BlockSpec(memory_space=pltpu.SMEM)],
        scratch_shapes=[pltpu.VMEM((BASE, cols), jnp.float32)] * 2,
        compiler_params=pltpu.CompilerParams(vmem_limit_bytes=VMEM),
        cost_estimate=pl.CostEstimate(flops=N * cols * 8, bytes_accessed=N * cols * 2, transcendentals=0),
        name="table",
    )(band_start)


def whiten_kernel(x_ref, table_ref, out_ref, acc):
    s = pl.program_id(0)

    @pl.when(s == 0)
    def _():
        acc[...] = jnp.zeros_like(acc)

    acc[...] += jnp.dot(x_ref[0], table_ref[...], preferred_element_type=jnp.float32)

    @pl.when(s == pl.num_programs(0) - 1)
    def _():
        copies, bands, chans, feats = out_ref.shape
        windows = feats // F
        low = lax.broadcasted_iota(jnp.int32, (chans, 128), 1) < F
        for k in range(bands // 2):
            white = []
            for w in range(windows):
                spec = acc[w * chans : (w + 1) * chans, k * 128 : (k + 1) * 128]
                square = spec * spec
                first = jnp.sum(jnp.where(low, square, 0.0), axis=1, keepdims=True)
                second = jnp.sum(jnp.where(low, 0.0, square), axis=1, keepdims=True)
                power = jnp.where(low, first, second) * (1.0 / F)
                white.append(spec * lax.rsqrt(power + 1e-06))
            for p in range(windows // 2):
                even, odd = white[2 * p], white[2 * p + 1]
                pair = (
                    jnp.where(low, even, pltpu.roll(odd, F, 1)),
                    jnp.where(low, pltpu.roll(even, F, 1), odd),
                )
                for h in range(2):
                    value = pair[h].astype(out_ref.dtype)
                    for c in range(copies):
                        out_ref[c, 2 * k + h, :, p * 128 : p * 128 + 128] = value


def whitened_blocks(x, table, copies, bands, chans, windows):
    ranges, rows, length = x.shape
    return pl.pallas_call(
        whiten_kernel,
        grid=(ranges,),
        out_shape=jax.ShapeDtypeStruct((copies, bands, chans, windows * F), jnp.bfloat16),
        in_specs=[
            pl.BlockSpec((1, rows, length), lambda s: (s, 0, 0)),
            pl.BlockSpec((length, bands * F), lambda s: (s, 0)),
        ],
        out_specs=pl.BlockSpec((copies, bands, chans, windows * F), lambda s: (0, 0, 0, 0)),
        scratch_shapes=[pltpu.VMEM((rows, bands * F), jnp.float32)],
        compiler_params=pltpu.CompilerParams(vmem_limit_bytes=VMEM),
        cost_estimate=pl.CostEstimate(
            flops=2 * ranges * rows * length * bands * F, bytes_accessed=6 * 1024 * 1024, transcendentals=0
        ),
        name="whiten",
    )(x, table)


def cross_kernel(place_ref, own_ref, other_ref, *rest):
    out_ref, stacked = rest[-2:]
    rows, feats = own_ref.shape[-2:]

    @pl.when(pl.program_id(0) == 0)
    def _():
        own = own_ref[0]
        stacked[:rows] = own
        first = lax.broadcasted_iota(jnp.int32, (rows, 128), 1) % F < K
        for k in range(feats // 128):
            at = slice(k * 128, k * 128 + 128)
            part = own[:, at].astype(jnp.float32)
            turned = jnp.where(first, pltpu.roll(part, 128 - K, 1), -pltpu.roll(part, K, 1))
            stacked[rows:, at] = turned.astype(stacked.dtype)

    product = lax.dot_general(
        stacked[...], other_ref[0], (((1,), (1,)), ((), ())), preferred_element_type=jnp.float32
    )
    product = (product * (1.0 / F)).astype(out_ref.dtype)
    out_ref[0, 0] = product[:rows]
    out_ref[0, 1] = product[rows:]


def cross(own, own_block, core, blocks, partial=None):
    count, rows, feats = blocks.shape
    place = jnp.stack([own_block, core]).astype(jnp.int32)
    in_specs = [
        pl.BlockSpec((1, rows, feats), lambda g, p: (p[0], 0, 0)),
        pl.BlockSpec((1, rows, feats), lambda g, p: (g, 0, 0)),
    ]
    args, aliases = [place, own, blocks], {}
    if partial is not None:
        in_specs.append(pl.BlockSpec(memory_space=pl.ANY))
        args.append(partial)
        aliases = {3: 0}
    return pl.pallas_call(
        cross_kernel,
        grid_spec=pltpu.PrefetchScalarGridSpec(
            num_scalar_prefetch=1,
            grid=(count,),
            in_specs=in_specs,
            out_specs=pl.BlockSpec((1, 2, rows, rows), lambda g, p: (0, 0, 0, 2 * g + p[1])),
            scratch_shapes=[pltpu.VMEM((2 * rows, feats), jnp.bfloat16)],
        ),
        out_shape=jax.ShapeDtypeStruct((1, 2, rows, 2 * count * rows), jnp.bfloat16),
        input_output_aliases=aliases,
        compiler_params=pltpu.CompilerParams(vmem_limit_bytes=VMEM),
        cost_estimate=pl.CostEstimate(
            flops=4 * count * rows * rows * feats, bytes_accessed=6 * 1024 * 1024, transcendentals=0
        ),
        name="cross",
    )(*args)


def shards(strain, band_start):
    chans, windows, length = strain.shape
    ranges = lax.axis_size(BAND)
    sub = chans // ranges
    n_y, n_zh = lax.axis_size("y"), lax.axis_size("zh")
    core = lax.axis_index("core")

    moved = lax.all_to_all(strain, BAND, 0, 0, tiled=True)
    table = make_table(band_start)
    x = moved.reshape(ranges, sub, windows, length).transpose(0, 2, 1, 3).reshape(ranges, windows * sub, length)
    white = whitened_blocks(x, table, n_zh, ranges, sub, windows)
    feats = windows * F
    panel = lax.all_to_all(
        white.reshape(n_zh * ranges, sub, feats), ("zh",) + BAND, 0, 0, tiled=True
    ).reshape(n_zh * chans, feats)
    spread = jnp.broadcast_to(panel[None], (n_y,) + panel.shape)
    mine = lax.all_to_all(spread, "y", 0, 0, tiled=True).reshape(n_y * n_zh, chans, feats)
    theirs = lax.ppermute(mine, "core", [(0, 1), (1, 0)])
    own_block = lax.axis_index("y") * n_zh + lax.axis_index("zh")
    partial = cross(mine, own_block, core, mine)
    return cross(mine, own_block, 1 - core, theirs, partial)


def solution(mesh):
    parts = Mesh(mesh.devices.reshape(4, 4, 2, 4, 2), ("y", "zh", "core", "x", "zl"))
    return jax.shard_map(
        shards,
        mesh=parts,
        in_specs=(P(CHAN, None, BAND), P()),
        out_specs=P(BAND, None, CHAN, None),
        check_vma=False,
    )
```

```python
import functools
import math

import jax
import jax.numpy as jnp
from jax import lax
from jax.experimental import pallas as pl
from jax.experimental.pallas import tpu as pltpu
from jax.sharding import Mesh, PartitionSpec as P

N = 4096
K = 32
F = 2 * K
BASE = 64
SCALE = 16.0
VMEM = 48 * 1024 * 1024

CHAN = ("y", "zh", "core")
BAND = ("x", "zl")


def partial_kernel(scalars_ref, x_ref, out_ref, table):
    samples, cols = table.shape
    bands = cols // F
    windows = x_ref.shape[0]
    coarse_n = samples // BASE
    step = 2.0 * math.pi / N

    def angles(rows, number):
        lane = lax.broadcasted_iota(jnp.int32, (rows, cols), 1)
        freq = lane % K
        for b in range(bands):
            freq = freq + jnp.where(lane // F == b, scalars_ref[b], 0)
        return freq * number(lax.broadcasted_iota(jnp.int32, (rows, cols), 0)), lane

    first = scalars_ref[bands] * coarse_n
    coarse, _ = angles(coarse_n, lambda row: row + first)
    coarse = (coarse % (N // BASE) * BASE).astype(jnp.float32) * step
    fine, lane = angles(BASE, lambda row: row)
    fine = ((fine + lane // K % 2 * (N // 4)) % N).astype(jnp.float32) * step
    cos_coarse, sin_coarse = jnp.cos(coarse), jnp.sin(coarse)
    cos_fine, sin_fine = jnp.cos(fine), jnp.sin(fine)
    small = lax.broadcasted_iota(jnp.int32, (BASE, 128), 0).astype(jnp.float32) * step
    large = (lax.broadcasted_iota(jnp.int32, (coarse_n, 128), 0) + first).astype(jnp.float32) * (step * BASE)
    cos_small, sin_small = jnp.cos(small), jnp.sin(small)
    cos_large, sin_large = jnp.cos(large), jnp.sin(large)
    for c in range(coarse_n):
        row = slice(c, c + 1)
        taper = 0.5 - 0.5 * (cos_large[row] * cos_small - sin_large[row] * sin_small)
        for k in range(cols // 128):
            at = slice(k * 128, k * 128 + 128)
            value = cos_coarse[row, at] * cos_fine[:, at] - sin_coarse[row, at] * sin_fine[:, at]
            table[c * BASE : c * BASE + BASE, at] = (taper * value).astype(table.dtype)

    low = lax.broadcasted_iota(jnp.int32, (x_ref.shape[1], 128), 1) < F
    for p in range(windows // 2):
        even = jnp.dot(x_ref[2 * p], table[...], preferred_element_type=jnp.float32) * SCALE
        odd = jnp.dot(x_ref[2 * p + 1], table[...], preferred_element_type=jnp.float32) * SCALE
        to = slice(p * 128, p * 128 + 128)
        for k in range(bands // 2):
            at = slice(k * 128, k * 128 + 128)
            out_ref[2 * k, :, to] = jnp.where(low, even[:, at], pltpu.roll(odd[:, at], F, 1))
            out_ref[2 * k + 1, :, to] = jnp.where(low, pltpu.roll(even[:, at], F, 1), odd[:, at])


def partial_spectra(strain, band_start):
    chans, windows, samples = strain.shape
    bands = band_start.shape[0]
    scalars = jnp.concatenate([band_start, lax.axis_index(BAND)[None].astype(jnp.int32)])
    return pl.pallas_call(
        partial_kernel,
        out_shape=jax.ShapeDtypeStruct((bands, chans, windows * F), jnp.float32),
        in_specs=[pl.BlockSpec(memory_space=pltpu.SMEM), pl.BlockSpec(memory_space=pltpu.VMEM)],
        out_specs=pl.BlockSpec(memory_space=pltpu.VMEM),
        scratch_shapes=[pltpu.VMEM((samples, bands * F), jnp.bfloat16)],
        compiler_params=pltpu.CompilerParams(vmem_limit_bytes=VMEM),
        cost_estimate=pl.CostEstimate(
            flops=2 * chans * windows * samples * bands * F, bytes_accessed=4 * 1024 * 1024, transcendentals=0
        ),
        name="partial",
    )(scalars, strain.transpose(1, 0, 2))


def whiten_kernel(x_ref, out_ref):
    rows, cols = x_ref.shape
    low = lax.broadcasted_iota(jnp.int32, (rows, 128), 1) < F
    for p in range(cols // 128):
        at = slice(p * 128, p * 128 + 128)
        spec = x_ref[:, at]
        square = spec * spec
        first = jnp.sum(jnp.where(low, square, 0.0), axis=1, keepdims=True)
        second = jnp.sum(jnp.where(low, 0.0, square), axis=1, keepdims=True)
        power = jnp.where(low, first, second) * (1.0 / F)
        out_ref[:, at] = (spec * lax.rsqrt(power + 1e-06 * SCALE * SCALE)).astype(out_ref.dtype)


def whiten(spectrum):
    return pl.pallas_call(
        whiten_kernel,
        out_shape=jax.ShapeDtypeStruct(spectrum.shape, jnp.bfloat16),
        compiler_params=pltpu.CompilerParams(vmem_limit_bytes=VMEM),
        name="whiten",
    )(spectrum)


def cross_kernel(blocks, n_y, place_ref, own_ref, *rest):
    out_ref, stacked, slots, sems = rest[-4:]
    rows, feats = own_ref.shape
    n_zh = place_ref[3]

    own = own_ref[...]
    stacked[:rows] = own
    first = lax.broadcasted_iota(jnp.int32, (rows, 128), 1) % F < K
    for k in range(feats // 128):
        at = slice(k * 128, k * 128 + 128)
        part = own[:, at].astype(jnp.float32)
        turned = jnp.where(first, pltpu.roll(part, 128 - K, 1), -pltpu.roll(part, K, 1))
        stacked[rows:, at] = turned.astype(stacked.dtype)

    copies = []
    for at, (operand, block, offset, zh, other) in enumerate(blocks):
        product = lax.dot_general(
            stacked[...],
            rest[operand][block * rows : (block + 1) * rows],
            (((1,), (1,)), ((), ())),
            preferred_element_type=jnp.float32,
        )
        product = (product * (1.0 / F)).astype(out_ref.dtype)
        slots[at, 0] = product[:rows]
        slots[at, 1] = product[rows:]
        core = 1 - place_ref[2] if other else place_ref[2]
        column = (((place_ref[0] + offset) % n_y) * n_zh + zh) * 2 + core
        columns = pl.ds(pl.multiple_of(column * rows, rows), rows)
        copies.append(pltpu.make_async_copy(slots.at[at], out_ref.at[0, :, :, columns], sems.at[at]))
        copies[-1].start()
    for copy in copies:
        copy.wait()


def cross(place, own, pieces, n_y, partial):
    rows, feats = own.shape
    blocks, args = [], []
    for i, (piece, offset, zh, other) in enumerate(pieces):
        args.append(piece)
        blocks += [(i, j, offset, zh + j, other) for j in range(piece.shape[0] // rows)]
    in_specs = [pl.BlockSpec(memory_space=pltpu.SMEM)] + [pl.BlockSpec(memory_space=pltpu.VMEM)] * (1 + len(args))
    aliases = {}
    if partial is None:
        shape = None
    else:
        args.append(partial)
        in_specs.append(pl.BlockSpec(memory_space=pl.ANY))
        aliases = {len(args) + 1: 0}
    return pl.pallas_call(
        functools.partial(cross_kernel, blocks, n_y),
        in_specs=in_specs,
        out_specs=pl.BlockSpec(memory_space=pl.ANY),
        scratch_shapes=[
            pltpu.VMEM((2 * rows, feats), jnp.bfloat16),
            pltpu.VMEM((len(blocks), 2, rows, rows), jnp.bfloat16),
            pltpu.SemaphoreType.DMA((len(blocks),)),
        ],
        out_shape=jax.ShapeDtypeStruct((1, 2, rows, 32 * rows), jnp.bfloat16),
        input_output_aliases=aliases,
        compiler_params=pltpu.CompilerParams(vmem_limit_bytes=VMEM),
        cost_estimate=pl.CostEstimate(
            flops=4 * len(blocks) * rows * rows * feats * 2,
            bytes_accessed=len(blocks) * 384 * 1024,
            transcendentals=0,
        ),
        name="cross",
    )(place, own, *args)


def shards(strain, band_start):
    n_y, n_zh = lax.axis_size("y"), lax.axis_size("zh")
    y, zh, core = lax.axis_index("y"), lax.axis_index("zh"), lax.axis_index("core")
    place = jnp.stack([y, zh, core, n_zh]).astype(jnp.int32)

    def turn(piece, by):
        return lax.ppermute(piece, "y", [(i, (i + by) % n_y) for i in range(n_y)])

    def swap(piece):
        return lax.ppermute(piece, "core", [(0, 1), (1, 0)])

    sums = partial_spectra(strain, band_start).astype(jnp.float16)
    moved = lax.all_to_all(sums, BAND, 0, 0, tiled=True)
    own = whiten(jnp.sum(moved.astype(jnp.float32), axis=0))
    chans = own.shape[0]
    panel = lax.all_gather(own, "zh", axis=0, tiled=True)

    half = panel.shape[0] // 2
    zh_half = n_zh // 2
    top, bottom = panel[:half], panel[half:]
    back_top, ahead_bottom = turn(top, 1), turn(bottom, -1)
    back_bottom, ahead_top = turn(bottom, 1), turn(top, -1)
    far_top, far_bottom = turn(back_top, 1), turn(ahead_bottom, -1)
    out = None
    for group in (
        [(panel, 0, 0)],
        [(back_top, -1, 0), (ahead_bottom, 1, zh_half), (back_bottom, -1, zh_half), (ahead_top, 1, 0)],
        [(far_top, 2, 0), (far_bottom, 2, zh_half)],
    ):
        pieces = [(piece, offset % n_y, first, False) for piece, offset, first in group]
        pieces += [(swap(piece), offset, first, True) for piece, offset, first, _ in pieces]
        out = cross(place, own, pieces, n_y, out)
    return out


def solution(mesh):
    parts = Mesh(mesh.devices.reshape(4, 4, 2, 4, 2), ("y", "zh", "core", "x", "zl"))
    return jax.shard_map(
        shards,
        mesh=parts,
        in_specs=(P(CHAN, None, BAND), P()),
        out_specs=P(BAND, None, CHAN, None),
        check_vma=False,
    )
```

```python
import functools
import math

import jax
import jax.numpy as jnp
from jax import lax
from jax.experimental import pallas as pl
from jax.experimental.pallas import tpu as pltpu
from jax.sharding import Mesh, PartitionSpec as P

N = 4096
K = 32
F = 2 * K
BASE = 32
SCALE = 16.0
VMEM = 48 * 1024 * 1024

CHAN = ("y", "zh", "core")
BAND = ("x", "zl")


def partial_kernel(scalars_ref, x_ref, out_ref, table):
    samples, cols = table.shape
    bands = cols // F
    coarse_n = samples // BASE
    step = 2.0 * math.pi / N

    def angles(rows, number):
        lane = lax.broadcasted_iota(jnp.int32, (rows, cols), 1)
        freq = lane % K
        for b in range(bands):
            freq = freq + jnp.where(lane // F == b, scalars_ref[b], 0)
        return freq * number(lax.broadcasted_iota(jnp.int32, (rows, cols), 0)), lane

    first = scalars_ref[bands] * coarse_n
    coarse, _ = angles(coarse_n, lambda row: row + first)
    coarse = (coarse % (N // BASE) * BASE).astype(jnp.float32) * step
    fine, lane = angles(BASE, lambda row: row)
    fine = ((fine + lane // K % 2 * (N // 4)) % N).astype(jnp.float32) * step
    cos_coarse, sin_coarse = jnp.cos(coarse), jnp.sin(coarse)
    cos_fine, sin_fine = jnp.cos(fine), jnp.sin(fine)
    small = lax.broadcasted_iota(jnp.int32, (BASE, 128), 0).astype(jnp.float32) * step
    large = (lax.broadcasted_iota(jnp.int32, (coarse_n, 128), 0) + first).astype(jnp.float32) * (step * BASE)
    cos_small, sin_small = jnp.cos(small), jnp.sin(small)
    cos_large, sin_large = jnp.cos(large), jnp.sin(large)
    for c in range(coarse_n):
        row = slice(c, c + 1)
        taper = 0.5 - 0.5 * (cos_large[row] * cos_small - sin_large[row] * sin_small)
        for k in range(cols // 128):
            at = slice(k * 128, k * 128 + 128)
            value = cos_coarse[row, at] * cos_fine[:, at] - sin_coarse[row, at] * sin_fine[:, at]
            table[c * BASE : c * BASE + BASE, at] = (taper * value).astype(table.dtype)

    windows, chans, _ = x_ref.shape
    low = lax.broadcasted_iota(jnp.int32, (chans, 128), 1) < F
    for p in range(windows // 2):
        even = jnp.dot(x_ref[2 * p], table[...], preferred_element_type=jnp.float32) * SCALE
        odd = jnp.dot(x_ref[2 * p + 1], table[...], preferred_element_type=jnp.float32) * SCALE
        to = slice(p * 128, p * 128 + 128)
        for k in range(bands // 2):
            at = slice(k * 128, k * 128 + 128)
            out_ref[2 * k, :, to] = jnp.where(low, even[:, at], pltpu.roll(odd[:, at], F, 1))
            out_ref[2 * k + 1, :, to] = jnp.where(low, pltpu.roll(even[:, at], F, 1), odd[:, at])


def partial_spectra(strain, band_start):
    chans, windows, samples = strain.shape
    bands = band_start.shape[0]
    scalars = jnp.concatenate([band_start, lax.axis_index(BAND)[None].astype(jnp.int32)])
    return pl.pallas_call(
        partial_kernel,
        out_shape=jax.ShapeDtypeStruct((bands, chans, windows * F), jnp.float32),
        in_specs=[pl.BlockSpec(memory_space=pltpu.SMEM), pl.BlockSpec(memory_space=pltpu.VMEM)],
        out_specs=pl.BlockSpec(memory_space=pltpu.VMEM),
        scratch_shapes=[pltpu.VMEM((samples, bands * F), jnp.bfloat16)],
        compiler_params=pltpu.CompilerParams(vmem_limit_bytes=VMEM),
        cost_estimate=pl.CostEstimate(
            flops=2 * chans * windows * samples * bands * F, bytes_accessed=4 * 1024 * 1024, transcendentals=0
        ),
        name="partial",
    )(scalars, strain.transpose(1, 0, 2))


def whiten_kernel(x_ref, out_ref, stacked_ref):
    rows, cols = x_ref.shape
    lane = lax.broadcasted_iota(jnp.int32, (rows, 128), 1)
    low, real = lane < F, lane % F < K
    for p in range(cols // 128):
        at = slice(p * 128, p * 128 + 128)
        spec = x_ref[:, at]
        square = spec * spec
        first = jnp.sum(jnp.where(low, square, 0.0), axis=1, keepdims=True)
        second = jnp.sum(jnp.where(low, 0.0, square), axis=1, keepdims=True)
        power = jnp.where(low, first, second) * (1.0 / F)
        white = spec * lax.rsqrt(power + 1e-06 * SCALE * SCALE)
        turned = jnp.where(real, pltpu.roll(white, 128 - K, 1), -pltpu.roll(white, K, 1))
        out_ref[:, at] = white.astype(out_ref.dtype)
        stacked_ref[:rows, at] = white.astype(out_ref.dtype)
        stacked_ref[rows:, at] = turned.astype(out_ref.dtype)


def whiten(spectrum):
    rows, cols = spectrum.shape
    return pl.pallas_call(
        whiten_kernel,
        out_shape=[
            jax.ShapeDtypeStruct((rows, cols), jnp.bfloat16),
            jax.ShapeDtypeStruct((2 * rows, cols), jnp.bfloat16),
        ],
        compiler_params=pltpu.CompilerParams(vmem_limit_bytes=VMEM),
        name="whiten",
    )(spectrum)


def cross_kernel(blocks, n_y, place_ref, stacked_ref, *rest):
    out_ref, slots, sems = rest[-3:]
    rows = stacked_ref.shape[0] // 2
    n_zh = place_ref[3]
    copies = []
    for at, (operand, block, offset, zh, other) in enumerate(blocks):
        product = lax.dot_general(
            stacked_ref[...],
            rest[operand][block * rows : (block + 1) * rows],
            (((1,), (1,)), ((), ())),
            preferred_element_type=jnp.float32,
        )
        product = (product * (1.0 / F)).astype(out_ref.dtype)
        slots[at, 0] = product[:rows]
        slots[at, 1] = product[rows:]
        core = 1 - place_ref[2] if other else place_ref[2]
        column = (((place_ref[0] + offset) % n_y) * n_zh + zh) * 2 + core
        columns = pl.ds(pl.multiple_of(column * rows, rows), rows)
        copies.append(pltpu.make_async_copy(slots.at[at], out_ref.at[0, :, :, columns], sems.at[at]))
        copies[-1].start()
    for copy in copies:
        copy.wait()


def cross(place, stacked, pieces, n_y, total, partial):
    rows, feats = stacked.shape[0] // 2, stacked.shape[1]
    blocks, args = [], []
    for i, (piece, places) in enumerate(pieces):
        args.append(piece)
        blocks += [(i, j) + where for j, where in enumerate(places)]
    in_specs = [pl.BlockSpec(memory_space=pltpu.SMEM)] + [pl.BlockSpec(memory_space=pltpu.VMEM)] * (1 + len(args))
    aliases = {}
    if partial is not None:
        args.append(partial)
        in_specs.append(pl.BlockSpec(memory_space=pl.ANY))
        aliases = {len(args) + 1: 0}
    return pl.pallas_call(
        functools.partial(cross_kernel, blocks, n_y),
        in_specs=in_specs,
        out_specs=pl.BlockSpec(memory_space=pl.ANY),
        scratch_shapes=[
            pltpu.VMEM((len(blocks), 2, rows, rows), jnp.bfloat16),
            pltpu.SemaphoreType.DMA((len(blocks),)),
        ],
        out_shape=jax.ShapeDtypeStruct((1, 2, rows, total * rows), jnp.bfloat16),
        input_output_aliases=aliases,
        compiler_params=pltpu.CompilerParams(vmem_limit_bytes=VMEM),
        cost_estimate=pl.CostEstimate(flops=len(blocks), bytes_accessed=len(blocks), transcendentals=0),
        name="cross",
    )(place, stacked, *args)


def shards(strain, band_start):
    n_y, n_zh = lax.axis_size("y"), lax.axis_size("zh")
    y, zh, core = lax.axis_index("y"), lax.axis_index("zh"), lax.axis_index("core")
    total = n_y * n_zh * lax.axis_size("core")
    place = jnp.stack([y, zh, core, n_zh]).astype(jnp.int32)

    def turn(piece, by):
        return lax.ppermute(piece, "y", [(i, (i + by) % n_y) for i in range(n_y)])

    def swap(piece):
        return lax.ppermute(piece, "core", [(0, 1), (1, 0)])

    sums = partial_spectra(strain, band_start).astype(jnp.float16)
    moved = lax.all_to_all(sums, BAND, 0, 0, tiled=True)
    own, stacked = whiten(jnp.sum(moved.astype(jnp.float32), axis=0))
    chans = own.shape[0]
    panel = lax.all_gather(own, "zh", axis=0, tiled=True)

    half = panel.shape[0] // 2
    zh_half = n_zh // 2
    top, bottom = panel[:half], panel[half:]
    back_top, ahead_bottom = turn(top, 1), turn(bottom, -1)
    back_bottom, ahead_top = turn(bottom, 1), turn(top, -1)
    far_top, far_bottom = turn(back_top, 1), turn(ahead_bottom, -1)
    swapped = swap(panel)

    def blocks(other):
        near_blocks = [(n_y - 1, z) for z in range(zh_half)] + [(1, z) for z in range(zh_half, n_zh)]
        near_blocks += [(n_y - 1, z) for z in range(zh_half, n_zh)] + [(1, z) for z in range(zh_half)]
        return (
            [(0, z, other) for z in range(n_zh)],
            [(offset, z, other) for offset, z in near_blocks],
            [(2, z, other) for z in range(n_zh)],
        )

    here, near_here, far_here = blocks(False)
    there, near_there, far_there = blocks(True)
    out = cross(place, stacked, [(panel, here)], n_y, total, None)
    back_bottom, ahead_top, out = lax.optimization_barrier((back_bottom, ahead_top, out))
    near = jnp.concatenate([back_top, ahead_bottom, back_bottom, ahead_top])
    out = cross(place, stacked, [(swapped, there), (near, near_here)], n_y, total, out)
    far_top, far_bottom, out = lax.optimization_barrier((far_top, far_bottom, out))
    rest = jnp.concatenate([near, far_top, far_bottom])
    rest_swapped = swap(rest)
    out = cross(place, stacked, [(far_top, far_here[:zh_half]), (far_bottom, far_here[zh_half:])], n_y, total, out)
    return cross(place, stacked, [(rest_swapped, near_there + far_there)], n_y, total, out)


def solution(mesh):
    parts = Mesh(mesh.devices.reshape(4, 4, 2, 4, 2), ("y", "zh", "core", "x", "zl"))
    return jax.shard_map(
        shards,
        mesh=parts,
        in_specs=(P(CHAN, None, BAND), P()),
        out_specs=P(BAND, None, CHAN, None),
        check_vma=False,
    )
```

```python
import functools
import math

import jax
import jax.numpy as jnp
from jax import lax
from jax.experimental import pallas as pl
from jax.experimental.pallas import tpu as pltpu
from jax.sharding import Mesh, PartitionSpec as P

N = 4096
K = 32
F = 2 * K
BASE = 32
SCALE = 16.0
VMEM = 48 * 1024 * 1024

CHAN = ("y", "zh", "core")
BAND = ("x", "zl")


def cos_sin(phase):
    quarter = (phase + N // 8) // (N // 4)
    x = (phase - quarter * (N // 4)).astype(jnp.float32) * (2.0 * math.pi / N)
    xx = x * x
    cos, sin = 1.0 / math.factorial(10), 1.0 / math.factorial(9)
    cos = -cos * xx + 1.0 / math.factorial(8)
    for k in (6, 4, 2, 0):
        cos = cos * xx + (-1.0) ** (k // 2) / math.factorial(k)
    sin = sin * xx - 1.0 / math.factorial(7)
    for k in (5, 3, 1):
        sin = sin * xx + (-1.0) ** (k // 2) / math.factorial(k)
    sin = sin * x
    odd, back = quarter % 2 == 1, quarter % 4 >= 2
    turned_cos, turned_sin = jnp.where(odd, -sin, cos), jnp.where(odd, cos, sin)
    return jnp.where(back, -turned_cos, turned_cos), jnp.where(back, -turned_sin, turned_sin)


def partial_kernel(scalars_ref, x_ref, out_ref, table):
    samples, cols = table.shape
    bands = cols // F
    coarse_n = samples // BASE

    def angles(rows, number):
        lane = lax.broadcasted_iota(jnp.int32, (rows, cols), 1)
        freq = lane % K
        for b in range(bands):
            freq = freq + jnp.where(lane // F == b, scalars_ref[b], 0)
        return freq * number(lax.broadcasted_iota(jnp.int32, (rows, cols), 0)), lane

    first = scalars_ref[bands] * coarse_n
    coarse, _ = angles(coarse_n, lambda row: row + first)
    cos_coarse, sin_coarse = cos_sin(coarse * BASE)
    fine, lane = angles(BASE, lambda row: row)
    cos_fine, sin_fine = cos_sin(fine + lane // K % 2 * (N // 4))
    cos_small, sin_small = cos_sin(lax.broadcasted_iota(jnp.int32, (BASE, 128), 0))
    cos_large, sin_large = cos_sin((lax.broadcasted_iota(jnp.int32, (coarse_n, 128), 0) + first) * BASE)
    for c in range(coarse_n):
        row = slice(c, c + 1)
        taper = 0.5 - 0.5 * (cos_large[row] * cos_small - sin_large[row] * sin_small)
        for k in range(cols // 128):
            at = slice(k * 128, k * 128 + 128)
            value = cos_coarse[row, at] * cos_fine[:, at] - sin_coarse[row, at] * sin_fine[:, at]
            table[c * BASE : c * BASE + BASE, at] = (taper * value).astype(table.dtype)

    windows, chans, _ = x_ref.shape
    low = lax.broadcasted_iota(jnp.int32, (chans, 128), 1) < F
    for p in range(windows // 2):
        even = jnp.dot(x_ref[2 * p], table[...], preferred_element_type=jnp.float32) * SCALE
        odd = jnp.dot(x_ref[2 * p + 1], table[...], preferred_element_type=jnp.float32) * SCALE
        to = slice(p * 128, p * 128 + 128)
        for k in range(bands // 2):
            at = slice(k * 128, k * 128 + 128)
            out_ref[2 * k, :, to] = jnp.where(low, even[:, at], pltpu.roll(odd[:, at], F, 1))
            out_ref[2 * k + 1, :, to] = jnp.where(low, pltpu.roll(even[:, at], F, 1), odd[:, at])


def partial_spectra(strain, band_start):
    chans, windows, samples = strain.shape
    bands = band_start.shape[0]
    scalars = jnp.concatenate([band_start, lax.axis_index(BAND)[None].astype(jnp.int32)])
    return pl.pallas_call(
        partial_kernel,
        out_shape=jax.ShapeDtypeStruct((bands, chans, windows * F), jnp.float32),
        in_specs=[pl.BlockSpec(memory_space=pltpu.SMEM), pl.BlockSpec(memory_space=pltpu.VMEM)],
        out_specs=pl.BlockSpec(memory_space=pltpu.VMEM),
        scratch_shapes=[pltpu.VMEM((samples, bands * F), jnp.bfloat16)],
        compiler_params=pltpu.CompilerParams(vmem_limit_bytes=VMEM),
        cost_estimate=pl.CostEstimate(
            flops=2 * chans * windows * samples * bands * F, bytes_accessed=4 * 1024 * 1024, transcendentals=0
        ),
        name="partial",
    )(scalars, strain.transpose(1, 0, 2))


def whiten_kernel(x_ref, out_ref, stacked_ref):
    rows, cols = x_ref.shape
    lane = lax.broadcasted_iota(jnp.int32, (rows, 128), 1)
    low, real = lane < F, lane % F < K
    for p in range(cols // 128):
        at = slice(p * 128, p * 128 + 128)
        spec = x_ref[:, at]
        square = spec * spec
        first = jnp.sum(jnp.where(low, square, 0.0), axis=1, keepdims=True)
        second = jnp.sum(jnp.where(low, 0.0, square), axis=1, keepdims=True)
        power = jnp.where(low, first, second) * (1.0 / F)
        white = spec * lax.rsqrt(power + 1e-06 * SCALE * SCALE)
        turned = jnp.where(real, pltpu.roll(white, 128 - K, 1), -pltpu.roll(white, K, 1))
        out_ref[:, at] = white.astype(out_ref.dtype)
        stacked_ref[:rows, at] = white.astype(out_ref.dtype)
        stacked_ref[rows:, at] = turned.astype(out_ref.dtype)


def whiten(spectrum):
    rows, cols = spectrum.shape
    return pl.pallas_call(
        whiten_kernel,
        out_shape=[
            jax.ShapeDtypeStruct((rows, cols), jnp.bfloat16),
            jax.ShapeDtypeStruct((2 * rows, cols), jnp.bfloat16),
        ],
        compiler_params=pltpu.CompilerParams(vmem_limit_bytes=VMEM),
        name="whiten",
    )(spectrum)


def cross_kernel(blocks, n_y, place_ref, stacked_ref, *rest):
    out_ref, slots, sems = rest[-3:]
    rows = stacked_ref.shape[0] // 2
    n_zh = place_ref[3]
    copies = []
    for at, (operand, block, offset, zh, other) in enumerate(blocks):
        product = lax.dot_general(
            stacked_ref[...],
            rest[operand][block * rows : (block + 1) * rows],
            (((1,), (1,)), ((), ())),
            preferred_element_type=jnp.float32,
        )
        product = (product * (1.0 / F)).astype(out_ref.dtype)
        slots[at, 0] = product[:rows]
        slots[at, 1] = product[rows:]
        core = 1 - place_ref[2] if other else place_ref[2]
        column = (((place_ref[0] + offset) % n_y) * n_zh + zh) * 2 + core
        columns = pl.ds(pl.multiple_of(column * rows, rows), rows)
        copies.append(pltpu.make_async_copy(slots.at[at], out_ref.at[0, :, :, columns], sems.at[at]))
        copies[-1].start()
    for copy in copies:
        copy.wait()


def cross(place, stacked, pieces, n_y, total, partial):
    rows, feats = stacked.shape[0] // 2, stacked.shape[1]
    blocks, args = [], []
    for i, (piece, places) in enumerate(pieces):
        args.append(piece)
        blocks += [(i, j) + where for j, where in enumerate(places)]
    in_specs = [pl.BlockSpec(memory_space=pltpu.SMEM)] + [pl.BlockSpec(memory_space=pltpu.VMEM)] * (1 + len(args))
    aliases = {}
    if partial is not None:
        args.append(partial)
        in_specs.append(pl.BlockSpec(memory_space=pl.ANY))
        aliases = {len(args) + 1: 0}
    return pl.pallas_call(
        functools.partial(cross_kernel, blocks, n_y),
        in_specs=in_specs,
        out_specs=pl.BlockSpec(memory_space=pl.ANY),
        scratch_shapes=[
            pltpu.VMEM((len(blocks), 2, rows, rows), jnp.bfloat16),
            pltpu.SemaphoreType.DMA((len(blocks),)),
        ],
        out_shape=jax.ShapeDtypeStruct((1, 2, rows, total * rows), jnp.bfloat16),
        input_output_aliases=aliases,
        compiler_params=pltpu.CompilerParams(vmem_limit_bytes=VMEM),
        cost_estimate=pl.CostEstimate(flops=len(blocks), bytes_accessed=len(blocks), transcendentals=0),
        name="cross",
    )(place, stacked, *args)


def shards(strain, band_start):
    n_y, n_zh = lax.axis_size("y"), lax.axis_size("zh")
    y, zh, core = lax.axis_index("y"), lax.axis_index("zh"), lax.axis_index("core")
    total = n_y * n_zh * lax.axis_size("core")
    place = jnp.stack([y, zh, core, n_zh]).astype(jnp.int32)

    def turn(piece, by):
        return lax.ppermute(piece, "y", [(i, (i + by) % n_y) for i in range(n_y)])

    def swap(piece):
        return lax.ppermute(piece, "core", [(0, 1), (1, 0)])

    sums = partial_spectra(strain, band_start).astype(jnp.float16)
    moved = lax.all_to_all(sums, BAND, 0, 0, tiled=True)
    own, stacked = whiten(jnp.sum(moved.astype(jnp.float32), axis=0))
    chans = own.shape[0]
    panel = lax.all_gather(own, "zh", axis=0, tiled=True)

    half = panel.shape[0] // 2
    zh_half = n_zh // 2
    top, bottom = panel[:half], panel[half:]
    back_top, ahead_bottom = turn(top, 1), turn(bottom, -1)
    far_top, far_bottom = turn(back_top, 1), turn(ahead_bottom, -1)
    swapped = swap(panel)

    def blocks(other):
        near_blocks = [(n_y - 1, z) for z in range(zh_half)] + [(1, z) for z in range(zh_half, n_zh)]
        near_blocks += [(n_y - 1, z) for z in range(zh_half, n_zh)] + [(1, z) for z in range(zh_half)]
        return (
            [(0, z, other) for z in range(n_zh)],
            [(offset, z, other) for offset, z in near_blocks],
            [(2, z, other) for z in range(n_zh)],
        )

    here, near_here, far_here = blocks(False)
    there, near_there, far_there = blocks(True)
    out = cross(place, stacked, [(panel, here)], n_y, total, None)
    top, bottom, out = lax.optimization_barrier((top, bottom, out))
    back_bottom, ahead_top = turn(bottom, 1), turn(top, -1)
    near = jnp.concatenate([back_top, ahead_bottom, back_bottom, ahead_top])
    out = cross(place, stacked, [(swapped, there), (near, near_here)], n_y, total, out)
    first, second, out = lax.optimization_barrier((near[: 2 * half], near[2 * half :], out))
    near_pieces = [(swap(first), near_there[:n_zh]), (swap(second), near_there[n_zh:])]
    far_top, far_bottom, out = lax.optimization_barrier((far_top, far_bottom, out))
    far_swapped = swap(jnp.concatenate([far_top, far_bottom]))
    pieces = near_pieces + [(far_top, far_here[:zh_half]), (far_bottom, far_here[zh_half:])]
    out = cross(place, stacked, pieces, n_y, total, out)
    return cross(place, stacked, [(far_swapped, far_there)], n_y, total, out)


def solution(mesh):
    parts = Mesh(mesh.devices.reshape(4, 4, 2, 4, 2), ("y", "zh", "core", "x", "zl"))
    return jax.shard_map(
        shards,
        mesh=parts,
        in_specs=(P(CHAN, None, BAND), P()),
        out_specs=P(BAND, None, CHAN, None),
        check_vma=False,
    )
```

```python
import functools
import math

import jax
import jax.numpy as jnp
from jax import lax
from jax.experimental import pallas as pl
from jax.experimental.pallas import tpu as pltpu
from jax.sharding import Mesh, PartitionSpec as P

N = 4096
K = 32
F = 2 * K
BASE = 32
SCALE = 16.0
VMEM = 48 * 1024 * 1024

CHAN = ("y", "zh", "core")
BAND = ("x", "zl")


def cos_sin(phase):
    quarter = (phase + N // 8) // (N // 4)
    x = (phase - quarter * (N // 4)).astype(jnp.float32) * (2.0 * math.pi / N)
    xx = x * x
    cos, sin = 1.0 / math.factorial(10), 1.0 / math.factorial(9)
    cos = -cos * xx + 1.0 / math.factorial(8)
    for k in (6, 4, 2, 0):
        cos = cos * xx + (-1.0) ** (k // 2) / math.factorial(k)
    sin = sin * xx - 1.0 / math.factorial(7)
    for k in (5, 3, 1):
        sin = sin * xx + (-1.0) ** (k // 2) / math.factorial(k)
    sin = sin * x
    odd, back = quarter % 2 == 1, quarter % 4 >= 2
    turned_cos, turned_sin = jnp.where(odd, -sin, cos), jnp.where(odd, cos, sin)
    return jnp.where(back, -turned_cos, turned_cos), jnp.where(back, -turned_sin, turned_sin)


def table_kernel(start_ref, strain_ref, table, strain_out, start, sems):
    first_copy = pltpu.make_async_copy(start_ref, start, sems.at[0])
    first_copy.start()
    count = sems.shape[0] - 1
    rows = strain_ref.shape[0] // count
    copies = []
    for i in range(count):
        part = pl.ds(i * rows, rows)
        copies.append(pltpu.make_async_copy(strain_ref.at[part], strain_out.at[part], sems.at[1 + i]))
        copies[-1].start()
    first = lax.axis_index(BAND) * (table.shape[0] // BASE)
    cos_small, sin_small = cos_sin(lax.broadcasted_iota(jnp.int32, (BASE, 128), 0))
    cos_large, sin_large = cos_sin((lax.broadcasted_iota(jnp.int32, (table.shape[0] // BASE, 128), 0) + first) * BASE)
    first_copy.wait()
    samples, cols = table.shape
    bands = cols // F
    coarse_n = samples // BASE

    def angles(rows, number):
        lane = lax.broadcasted_iota(jnp.int32, (rows, cols), 1)
        freq = lane % K
        for b in range(bands):
            freq = freq + jnp.where(lane // F == b, start[b], 0)
        return freq * number(lax.broadcasted_iota(jnp.int32, (rows, cols), 0)), lane

    coarse, _ = angles(coarse_n, lambda row: row + first)
    cos_coarse, sin_coarse = cos_sin(coarse * BASE)
    fine, lane = angles(BASE, lambda row: row)
    cos_fine, sin_fine = cos_sin(fine + lane // K % 2 * (N // 4))
    for c in range(coarse_n):
        row = slice(c, c + 1)
        taper = 0.5 - 0.5 * (cos_large[row] * cos_small - sin_large[row] * sin_small)
        for k in range(cols // 128):
            at = slice(k * 128, k * 128 + 128)
            value = cos_coarse[row, at] * cos_fine[:, at] - sin_coarse[row, at] * sin_fine[:, at]
            table[c * BASE : c * BASE + BASE, at] = (taper * value).astype(table.dtype)
    for copy in copies:
        copy.wait()


def partial_kernel(x_ref, table, out_ref):
    bands = table.shape[1] // F
    windows, chans, _ = x_ref.shape
    low = lax.broadcasted_iota(jnp.int32, (chans, 128), 1) < F
    for p in range(windows // 2):
        even = jnp.dot(x_ref[2 * p], table[...], preferred_element_type=jnp.float32) * SCALE
        odd = jnp.dot(x_ref[2 * p + 1], table[...], preferred_element_type=jnp.float32) * SCALE
        to = slice(p * 128, p * 128 + 128)
        for k in range(bands // 2):
            at = slice(k * 128, k * 128 + 128)
            out_ref[2 * k, :, to] = jnp.where(low, even[:, at], pltpu.roll(odd[:, at], F, 1))
            out_ref[2 * k + 1, :, to] = jnp.where(low, pltpu.roll(even[:, at], F, 1), odd[:, at])


def partial_spectra(strain, band_start):
    chans, windows, samples = strain.shape
    bands = band_start.shape[0]
    table, strain = pl.pallas_call(
        table_kernel,
        out_shape=[
            jax.ShapeDtypeStruct((samples, bands * F), jnp.bfloat16),
            jax.ShapeDtypeStruct(strain.shape, strain.dtype),
        ],
        in_specs=[pl.BlockSpec(memory_space=pl.ANY)] * 2,
        scratch_shapes=[pltpu.SMEM(band_start.shape, jnp.int32), pltpu.SemaphoreType.DMA((9,))],
        compiler_params=pltpu.CompilerParams(vmem_limit_bytes=52 * 1024 * 1024),
        name="table",
    )(band_start, strain)
    return pl.pallas_call(
        partial_kernel,
        out_shape=jax.ShapeDtypeStruct((bands, chans, windows * F), jnp.float32),
        compiler_params=pltpu.CompilerParams(vmem_limit_bytes=VMEM),
        cost_estimate=pl.CostEstimate(
            flops=2 * chans * windows * samples * bands * F, bytes_accessed=4 * 1024 * 1024, transcendentals=0
        ),
        name="partial",
    )(strain.transpose(1, 0, 2), table)


def whiten_kernel(x_ref, out_ref):
    rows, cols = x_ref.shape
    low = lax.broadcasted_iota(jnp.int32, (rows, 128), 1) < F
    for p in range(cols // 128):
        at = slice(p * 128, p * 128 + 128)
        spec = x_ref[:, at]
        square = spec * spec
        first = jnp.sum(jnp.where(low, square, 0.0), axis=1, keepdims=True)
        second = jnp.sum(jnp.where(low, 0.0, square), axis=1, keepdims=True)
        power = jnp.where(low, first, second) * (1.0 / F)
        out_ref[:, at] = (spec * lax.rsqrt(power + 1e-06 * SCALE * SCALE)).astype(out_ref.dtype)


def whiten(spectrum):
    return pl.pallas_call(
        whiten_kernel,
        out_shape=jax.ShapeDtypeStruct(spectrum.shape, jnp.bfloat16),
        compiler_params=pltpu.CompilerParams(vmem_limit_bytes=VMEM),
        name="whiten",
    )(spectrum)


def first_cross_kernel(blocks, n_y, place_ref, own_ref, *rest):
    out_ref, stacked_ref, slots, sems = rest[-4:]
    rows, feats = own_ref.shape
    real = lax.broadcasted_iota(jnp.int32, (rows, 128), 1) % F < K
    stacked_ref[:rows] = own_ref[...]
    for k in range(feats // 128):
        at = slice(k * 128, k * 128 + 128)
        part = own_ref[:, at].astype(jnp.float32)
        turned = jnp.where(real, pltpu.roll(part, 128 - K, 1), -pltpu.roll(part, K, 1))
        stacked_ref[rows:, at] = turned.astype(stacked_ref.dtype)
    cross_kernel(blocks, n_y, place_ref, stacked_ref, *rest[:-4], out_ref, slots, sems)


def cross_kernel(blocks, n_y, place_ref, stacked_ref, *rest):
    out_ref, slots, sems = rest[-3:]
    rows = stacked_ref.shape[0] // 2
    n_zh = place_ref[3]
    copies = []
    for at, (operand, block, offset, zh, other) in enumerate(blocks):
        product = lax.dot_general(
            stacked_ref[...],
            rest[operand][block * rows : (block + 1) * rows],
            (((1,), (1,)), ((), ())),
            preferred_element_type=jnp.float32,
        )
        product = (product * (1.0 / F)).astype(out_ref.dtype)
        slots[at, 0] = product[:rows]
        slots[at, 1] = product[rows:]
        core = 1 - place_ref[2] if other else place_ref[2]
        column = (((place_ref[0] + offset) % n_y) * n_zh + zh) * 2 + core
        columns = pl.ds(pl.multiple_of(column * rows, rows), rows)
        copies.append(pltpu.make_async_copy(slots.at[at], out_ref.at[0, :, :, columns], sems.at[at]))
        copies[-1].start()
    for copy in copies:
        copy.wait()


def cross(place, stacked, pieces, n_y, total, partial):
    begin = partial is None
    rows, feats = stacked.shape[0] // (1 if begin else 2), stacked.shape[1]
    blocks, args = [], []
    for i, (piece, places) in enumerate(pieces):
        args.append(piece)
        blocks += [(i, j) + where for j, where in enumerate(places)]
    in_specs = [pl.BlockSpec(memory_space=pltpu.SMEM)] + [pl.BlockSpec(memory_space=pltpu.VMEM)] * (1 + len(args))
    out_specs = [pl.BlockSpec(memory_space=pl.ANY)]
    out_shape = [jax.ShapeDtypeStruct((1, 2, rows, total * rows), jnp.bfloat16)]
    aliases = {}
    if begin:
        out_specs.append(pl.BlockSpec(memory_space=pltpu.VMEM))
        out_shape.append(jax.ShapeDtypeStruct((2 * rows, feats), jnp.bfloat16))
    else:
        args.append(partial)
        in_specs.append(pl.BlockSpec(memory_space=pl.ANY))
        aliases = {len(args) + 1: 0}
    result = pl.pallas_call(
        functools.partial(first_cross_kernel if begin else cross_kernel, blocks, n_y),
        in_specs=in_specs,
        out_specs=out_specs,
        scratch_shapes=[
            pltpu.VMEM((len(blocks), 2, rows, rows), jnp.bfloat16),
            pltpu.SemaphoreType.DMA((len(blocks),)),
        ],
        out_shape=out_shape,
        input_output_aliases=aliases,
        compiler_params=pltpu.CompilerParams(vmem_limit_bytes=VMEM),
        cost_estimate=pl.CostEstimate(flops=len(blocks), bytes_accessed=len(blocks), transcendentals=0),
        name="cross",
    )(place, stacked, *args)
    return result if begin else result[0]


def shards(strain, band_start):
    n_y, n_zh = lax.axis_size("y"), lax.axis_size("zh")
    y, zh, core = lax.axis_index("y"), lax.axis_index("zh"), lax.axis_index("core")
    total = n_y * n_zh * lax.axis_size("core")
    place = jnp.stack([y, zh, core, n_zh]).astype(jnp.int32)

    def turn(piece, by):
        return lax.ppermute(piece, "y", [(i, (i + by) % n_y) for i in range(n_y)])

    def swap(piece):
        return lax.ppermute(piece, "core", [(0, 1), (1, 0)])

    sums = partial_spectra(strain, band_start).astype(jnp.float16)
    moved = lax.all_to_all(sums, BAND, 0, 0, tiled=True)
    own = whiten(jnp.sum(moved.astype(jnp.float32), axis=0))
    chans = own.shape[0]
    panel = lax.all_gather(own, "zh", axis=0, tiled=True)

    half = panel.shape[0] // 2
    zh_half = n_zh // 2
    top, bottom = panel[:half], panel[half:]
    back_top, ahead_bottom = turn(top, 1), turn(bottom, -1)
    far_top, far_bottom = turn(back_top, 1), turn(ahead_bottom, -1)
    swapped = swap(panel)

    def blocks(other):
        near_blocks = [(n_y - 1, z) for z in range(zh_half)] + [(1, z) for z in range(zh_half, n_zh)]
        near_blocks += [(n_y - 1, z) for z in range(zh_half, n_zh)] + [(1, z) for z in range(zh_half)]
        return (
            [(0, z, other) for z in range(n_zh)],
            [(offset, z, other) for offset, z in near_blocks],
            [(2, z, other) for z in range(n_zh)],
        )

    here, near_here, far_here = blocks(False)
    there, near_there, far_there = blocks(True)
    out, stacked = cross(place, own, [(panel, here)], n_y, total, None)
    top, bottom, out = lax.optimization_barrier((top, bottom, out))
    back_bottom, ahead_top = turn(bottom, 1), turn(top, -1)
    near = jnp.concatenate([back_top, ahead_bottom, back_bottom, ahead_top])
    out = cross(place, stacked, [(swapped, there), (near, near_here)], n_y, total, out)
    first, second, out = lax.optimization_barrier((near[: 2 * half], near[2 * half :], out))
    near_pieces = [(swap(first), near_there[:n_zh]), (swap(second), near_there[n_zh:])]
    far_top, far_bottom, out = lax.optimization_barrier((far_top, far_bottom, out))
    far_swapped = swap(jnp.concatenate([far_top, far_bottom]))
    pieces = near_pieces + [(far_top, far_here[:zh_half]), (far_bottom, far_here[zh_half:])]
    out = cross(place, stacked, pieces, n_y, total, out)
    return cross(place, stacked, [(far_swapped, far_there)], n_y, total, out)


def solution(mesh):
    parts = Mesh(mesh.devices.reshape(4, 4, 2, 4, 2), ("y", "zh", "core", "x", "zl"))
    return jax.shard_map(
        shards,
        mesh=parts,
        in_specs=(P(CHAN, None, BAND), P()),
        out_specs=P(BAND, None, CHAN, None),
        check_vma=False,
    )
```

```python
import functools
import math

import jax
import jax.numpy as jnp
from jax import lax
from jax.experimental import pallas as pl
from jax.experimental.pallas import tpu as pltpu
from jax.sharding import Mesh, PartitionSpec as P

N = 4096
K = 32
F = 2 * K
BASE = 32
SCALE = 16.0
VMEM = 48 * 1024 * 1024

CHAN = ("y", "zh", "core")
BAND = ("x", "zl")


def cos_sin(phase):
    quarter = (phase + N // 8) // (N // 4)
    x = (phase - quarter * (N // 4)).astype(jnp.float32) * (2.0 * math.pi / N)
    xx = x * x
    cos, sin = 1.0 / math.factorial(10), 1.0 / math.factorial(9)
    cos = -cos * xx + 1.0 / math.factorial(8)
    for k in (6, 4, 2, 0):
        cos = cos * xx + (-1.0) ** (k // 2) / math.factorial(k)
    sin = sin * xx - 1.0 / math.factorial(7)
    for k in (5, 3, 1):
        sin = sin * xx + (-1.0) ** (k // 2) / math.factorial(k)
    sin = sin * x
    odd, back = quarter % 2 == 1, quarter % 4 >= 2
    turned_cos, turned_sin = jnp.where(odd, -sin, cos), jnp.where(odd, cos, sin)
    return jnp.where(back, -turned_cos, turned_cos), jnp.where(back, -turned_sin, turned_sin)


def table_kernel(start_ref, strain_ref, table, strain_out, start, sems):
    first_copy = pltpu.make_async_copy(start_ref, start, sems.at[0])
    first_copy.start()
    count = sems.shape[0] - 1
    rows = strain_ref.shape[0] // count
    copies = []
    for i in range(count):
        part = pl.ds(i * rows, rows)
        copies.append(pltpu.make_async_copy(strain_ref.at[part], strain_out.at[part], sems.at[1 + i]))
        copies[-1].start()
    first = lax.axis_index(BAND) * (table.shape[0] // BASE)
    cos_small, sin_small = cos_sin(lax.broadcasted_iota(jnp.int32, (BASE, 128), 0))
    cos_large, sin_large = cos_sin((lax.broadcasted_iota(jnp.int32, (table.shape[0] // BASE, 128), 0) + first) * BASE)
    first_copy.wait()
    samples, cols = table.shape
    bands = cols // F
    coarse_n = samples // BASE

    def angles(rows, number):
        lane = lax.broadcasted_iota(jnp.int32, (rows, cols), 1)
        freq = lane % K
        for b in range(bands):
            freq = freq + jnp.where(lane // F == b, start[b], 0)
        return freq * number(lax.broadcasted_iota(jnp.int32, (rows, cols), 0)), lane

    coarse, _ = angles(coarse_n, lambda row: row + first)
    cos_coarse, sin_coarse = cos_sin(coarse * BASE)
    fine, lane = angles(BASE, lambda row: row)
    cos_fine, sin_fine = cos_sin(fine + lane // K % 2 * (N // 4))
    for c in range(coarse_n):
        row = slice(c, c + 1)
        taper = 0.5 - 0.5 * (cos_large[row] * cos_small - sin_large[row] * sin_small)
        for k in range(cols // 128):
            at = slice(k * 128, k * 128 + 128)
            value = cos_coarse[row, at] * cos_fine[:, at] - sin_coarse[row, at] * sin_fine[:, at]
            table[c * BASE : c * BASE + BASE, at] = (taper * value).astype(table.dtype)
    for copy in copies:
        copy.wait()


def partial_kernel(x_ref, table, out_ref):
    bands = table.shape[1] // F
    windows, chans, _ = x_ref.shape
    low = lax.broadcasted_iota(jnp.int32, (chans, 128), 1) < F
    for p in range(windows // 2):
        even = jnp.dot(x_ref[2 * p], table[...], preferred_element_type=jnp.float32) * SCALE
        odd = jnp.dot(x_ref[2 * p + 1], table[...], preferred_element_type=jnp.float32) * SCALE
        to = slice(p * 128, p * 128 + 128)
        for k in range(bands // 2):
            at = slice(k * 128, k * 128 + 128)
            out_ref[2 * k, :, to] = jnp.where(low, even[:, at], pltpu.roll(odd[:, at], F, 1))
            out_ref[2 * k + 1, :, to] = jnp.where(low, pltpu.roll(even[:, at], F, 1), odd[:, at])


def partial_spectra(strain, band_start):
    chans, windows, samples = strain.shape
    bands = band_start.shape[0]
    table, strain = pl.pallas_call(
        table_kernel,
        out_shape=[
            jax.ShapeDtypeStruct((samples, bands * F), jnp.bfloat16),
            jax.ShapeDtypeStruct(strain.shape, strain.dtype),
        ],
        in_specs=[pl.BlockSpec(memory_space=pl.ANY)] * 2,
        scratch_shapes=[pltpu.SMEM(band_start.shape, jnp.int32), pltpu.SemaphoreType.DMA((9,))],
        compiler_params=pltpu.CompilerParams(vmem_limit_bytes=52 * 1024 * 1024),
        name="table",
    )(band_start, strain)
    return pl.pallas_call(
        partial_kernel,
        out_shape=jax.ShapeDtypeStruct((bands, chans, windows * F), jnp.float32),
        compiler_params=pltpu.CompilerParams(vmem_limit_bytes=VMEM),
        cost_estimate=pl.CostEstimate(
            flops=2 * chans * windows * samples * bands * F, bytes_accessed=4 * 1024 * 1024, transcendentals=0
        ),
        name="partial",
    )(strain.transpose(1, 0, 2), table)


def whiten_kernel(x_ref, out_ref):
    rows, cols = x_ref.shape
    low = lax.broadcasted_iota(jnp.int32, (rows, 128), 1) < F
    for p in range(cols // 128):
        at = slice(p * 128, p * 128 + 128)
        spec = x_ref[:, at]
        square = spec * spec
        first = jnp.sum(jnp.where(low, square, 0.0), axis=1, keepdims=True)
        second = jnp.sum(jnp.where(low, 0.0, square), axis=1, keepdims=True)
        power = jnp.where(low, first, second) * (1.0 / F)
        out_ref[:, at] = (spec * lax.rsqrt(power + 1e-06 * SCALE * SCALE)).astype(out_ref.dtype)


def whiten(spectrum):
    return pl.pallas_call(
        whiten_kernel,
        out_shape=jax.ShapeDtypeStruct(spectrum.shape, jnp.bfloat16),
        compiler_params=pltpu.CompilerParams(vmem_limit_bytes=VMEM),
        name="whiten",
    )(spectrum)


def first_cross_kernel(blocks, own_ref, *rest):
    out_ref, stacked_ref, slots, sems = rest[-4:]
    rows, feats = own_ref.shape
    real = lax.broadcasted_iota(jnp.int32, (rows, 128), 1) % F < K
    stacked_ref[:rows] = own_ref[...]
    for k in range(feats // 128):
        at = slice(k * 128, k * 128 + 128)
        part = own_ref[:, at].astype(jnp.float32)
        turned = jnp.where(real, pltpu.roll(part, 128 - K, 1), -pltpu.roll(part, K, 1))
        stacked_ref[rows:, at] = turned.astype(stacked_ref.dtype)
    cross_kernel(blocks, stacked_ref, *rest[:-4], out_ref, slots, sems)


def cross_kernel(blocks, stacked_ref, *rest):
    out_ref, slots, sems = rest[-3:]
    rows = stacked_ref.shape[0] // 2
    n_y, n_zh = lax.axis_size("y"), lax.axis_size("zh")
    y, own_core = lax.axis_index("y"), lax.axis_index("core")
    copies = []
    for at, (operand, block, offset, zh, other) in enumerate(blocks):
        core = 1 - own_core if other else own_core
        column = ((y + offset) % n_y * n_zh + zh) * 2 + core
        columns = pl.ds(pl.multiple_of(column * rows, rows), rows)
        turned = rest[operand][block * rows : (block + 1) * rows].T
        for part in range(2):
            product = jnp.dot(stacked_ref[part * rows : (part + 1) * rows], turned, preferred_element_type=jnp.float32)
            slots[at, part] = (product * (1.0 / F)).astype(out_ref.dtype)
        copies.append(pltpu.make_async_copy(slots.at[at], out_ref.at[0, :, :, columns], sems.at[at]))
        copies[-1].start()
    for copy in copies:
        copy.wait()


def cross(stacked, pieces, total, partial):
    begin = partial is None
    rows, feats = stacked.shape[0] // (1 if begin else 2), stacked.shape[1]
    blocks, args = [], []
    for i, (piece, places) in enumerate(pieces):
        args.append(piece)
        blocks += [(i, j) + where for j, where in enumerate(places)]
    in_specs = [pl.BlockSpec(memory_space=pltpu.VMEM)] * (1 + len(args))
    out_specs = [pl.BlockSpec(memory_space=pl.ANY)]
    out_shape = [jax.ShapeDtypeStruct((1, 2, rows, total * rows), jnp.bfloat16)]
    aliases = {}
    if begin:
        out_specs.append(pl.BlockSpec(memory_space=pltpu.VMEM))
        out_shape.append(jax.ShapeDtypeStruct((2 * rows, feats), jnp.bfloat16))
    else:
        args.append(partial)
        in_specs.append(pl.BlockSpec(memory_space=pl.ANY))
        aliases = {len(args): 0}
    result = pl.pallas_call(
        functools.partial(first_cross_kernel if begin else cross_kernel, blocks),
        in_specs=in_specs,
        out_specs=out_specs,
        scratch_shapes=[
            pltpu.VMEM((len(blocks), 2, rows, rows), jnp.bfloat16),
            pltpu.SemaphoreType.DMA((len(blocks),)),
        ],
        out_shape=out_shape,
        input_output_aliases=aliases,
        compiler_params=pltpu.CompilerParams(vmem_limit_bytes=VMEM),
        cost_estimate=pl.CostEstimate(flops=len(blocks), bytes_accessed=len(blocks), transcendentals=0),
        name="cross",
    )(stacked, *args)
    return result if begin else result[0]


def shards(strain, band_start):
    n_y, n_zh = lax.axis_size("y"), lax.axis_size("zh")
    total = n_y * n_zh * lax.axis_size("core")

    def turn(piece, by):
        return lax.ppermute(piece, "y", [(i, (i + by) % n_y) for i in range(n_y)])

    def swap(piece):
        return lax.ppermute(piece, "core", [(0, 1), (1, 0)])

    sums = partial_spectra(strain, band_start).astype(jnp.float16)
    moved = lax.all_to_all(sums, BAND, 0, 0, tiled=True)
    own = whiten(jnp.sum(moved.astype(jnp.float32), axis=0))
    chans = own.shape[0]
    panel = lax.all_gather(own, "zh", axis=0, tiled=True)

    half = panel.shape[0] // 2
    zh_half = n_zh // 2
    top, bottom = panel[:half], panel[half:]
    back_top, ahead_bottom = turn(top, 1), turn(bottom, -1)
    far_top, far_bottom = turn(back_top, 1), turn(ahead_bottom, -1)
    swapped = swap(panel)

    def blocks(other):
        near_blocks = [(n_y - 1, z) for z in range(zh_half)] + [(1, z) for z in range(zh_half, n_zh)]
        near_blocks += [(n_y - 1, z) for z in range(zh_half, n_zh)] + [(1, z) for z in range(zh_half)]
        return (
            [(0, z, other) for z in range(n_zh)],
            [(offset, z, other) for offset, z in near_blocks],
            [(2, z, other) for z in range(n_zh)],
        )

    here, near_here, far_here = blocks(False)
    there, near_there, far_there = blocks(True)
    out, stacked = cross(own, [(panel, here)], total, None)
    top, bottom, out = lax.optimization_barrier((top, bottom, out))
    back_bottom, ahead_top = turn(bottom, 1), turn(top, -1)
    near = jnp.concatenate([back_top, ahead_bottom, back_bottom, ahead_top])
    out = cross(stacked, [(swapped, there), (near, near_here)], total, out)
    first, second, out = lax.optimization_barrier((near[: 2 * half], near[2 * half :], out))
    near_pieces = [(swap(first), near_there[:n_zh]), (swap(second), near_there[n_zh:])]
    far_top, far_bottom, out = lax.optimization_barrier((far_top, far_bottom, out))
    far_swapped = swap(jnp.concatenate([far_top, far_bottom]))
    pieces = near_pieces + [(far_top, far_here[:zh_half]), (far_bottom, far_here[zh_half:])]
    out = cross(stacked, pieces, total, out)
    return cross(stacked, [(far_swapped, far_there)], total, out)


def solution(mesh):
    parts = Mesh(mesh.devices.reshape(4, 4, 2, 4, 2), ("y", "zh", "core", "x", "zl"))
    return jax.shard_map(
        shards,
        mesh=parts,
        in_specs=(P(CHAN, None, BAND), P()),
        out_specs=P(BAND, None, CHAN, None),
        check_vma=False,
    )
```

```python
import functools
import math

import jax
import jax.numpy as jnp
from jax import lax
from jax.experimental import pallas as pl
from jax.experimental.pallas import tpu as pltpu
from jax.sharding import Mesh, PartitionSpec as P

N = 4096
K = 32
F = 2 * K
BASE = 32
SCALE = 16.0
VMEM = 48 * 1024 * 1024

CHAN = ("y", "zh", "core")
BAND = ("x", "zl")


def cos_sin(phase):
    quarter = (phase + N // 8) // (N // 4)
    x = (phase - quarter * (N // 4)).astype(jnp.float32) * (2.0 * math.pi / N)
    xx = x * x
    cos, sin = 1.0 / math.factorial(10), 1.0 / math.factorial(9)
    cos = -cos * xx + 1.0 / math.factorial(8)
    for k in (6, 4, 2, 0):
        cos = cos * xx + (-1.0) ** (k // 2) / math.factorial(k)
    sin = sin * xx - 1.0 / math.factorial(7)
    for k in (5, 3, 1):
        sin = sin * xx + (-1.0) ** (k // 2) / math.factorial(k)
    sin = sin * x
    odd, back = quarter % 2 == 1, quarter % 4 >= 2
    turned_cos, turned_sin = jnp.where(odd, -sin, cos), jnp.where(odd, cos, sin)
    return jnp.where(back, -turned_cos, turned_cos), jnp.where(back, -turned_sin, turned_sin)


def table_kernel(start_ref, strain_ref, table, strain_out, start, sems):
    first_copy = pltpu.make_async_copy(start_ref, start, sems.at[0])
    first_copy.start()
    count = sems.shape[0] - 1
    rows = strain_ref.shape[0] // count
    copies = []
    for i in range(count):
        part = pl.ds(i * rows, rows)
        copies.append(pltpu.make_async_copy(strain_ref.at[part], strain_out.at[part], sems.at[1 + i]))
        copies[-1].start()
    first = lax.axis_index(BAND) * (table.shape[0] // BASE)
    cos_small, sin_small = cos_sin(lax.broadcasted_iota(jnp.int32, (BASE, 128), 0))
    cos_large, sin_large = cos_sin((lax.broadcasted_iota(jnp.int32, (table.shape[0] // BASE, 128), 0) + first) * BASE)
    first_copy.wait()
    samples, cols = table.shape
    bands = cols // F
    coarse_n = samples // BASE

    def angles(rows, number):
        lane = lax.broadcasted_iota(jnp.int32, (rows, cols), 1)
        freq = lane % K
        for b in range(bands):
            freq = freq + jnp.where(lane // F == b, start[b], 0)
        return freq * number(lax.broadcasted_iota(jnp.int32, (rows, cols), 0)), lane

    coarse, _ = angles(coarse_n, lambda row: row + first)
    cos_coarse, sin_coarse = cos_sin(coarse * BASE)
    fine, lane = angles(BASE, lambda row: row)
    cos_fine, sin_fine = cos_sin(fine + lane // K % 2 * (N // 4))
    for c in range(coarse_n):
        row = slice(c, c + 1)
        taper = 0.5 - 0.5 * (cos_large[row] * cos_small - sin_large[row] * sin_small)
        for k in range(cols // 128):
            at = slice(k * 128, k * 128 + 128)
            value = cos_coarse[row, at] * cos_fine[:, at] - sin_coarse[row, at] * sin_fine[:, at]
            table[c * BASE : c * BASE + BASE, at] = (taper * value).astype(table.dtype)
    for copy in copies:
        copy.wait()


def partial_kernel(x_ref, table, out_ref):
    bands = table.shape[1] // F
    windows, chans, _ = x_ref.shape
    low = lax.broadcasted_iota(jnp.int32, (chans, 128), 1) < F
    for p in range(windows // 2):
        even = jnp.dot(x_ref[2 * p], table[...], preferred_element_type=jnp.float32) * SCALE
        odd = jnp.dot(x_ref[2 * p + 1], table[...], preferred_element_type=jnp.float32) * SCALE
        to = slice(p * 128, p * 128 + 128)
        for k in range(bands // 2):
            at = slice(k * 128, k * 128 + 128)
            out_ref[2 * k, :, to] = jnp.where(low, even[:, at], pltpu.roll(odd[:, at], F, 1))
            out_ref[2 * k + 1, :, to] = jnp.where(low, pltpu.roll(even[:, at], F, 1), odd[:, at])


def partial_spectra(strain, band_start):
    chans, windows, samples = strain.shape
    bands = band_start.shape[0]
    table, strain = pl.pallas_call(
        table_kernel,
        out_shape=[
            jax.ShapeDtypeStruct((samples, bands * F), jnp.bfloat16),
            jax.ShapeDtypeStruct(strain.shape, strain.dtype),
        ],
        in_specs=[pl.BlockSpec(memory_space=pl.ANY)] * 2,
        scratch_shapes=[pltpu.SMEM(band_start.shape, jnp.int32), pltpu.SemaphoreType.DMA((9,))],
        compiler_params=pltpu.CompilerParams(vmem_limit_bytes=52 * 1024 * 1024),
        name="table",
    )(band_start, strain)
    return pl.pallas_call(
        partial_kernel,
        out_shape=jax.ShapeDtypeStruct((bands, chans, windows * F), jnp.float32),
        compiler_params=pltpu.CompilerParams(vmem_limit_bytes=VMEM),
        cost_estimate=pl.CostEstimate(
            flops=2 * chans * windows * samples * bands * F, bytes_accessed=4 * 1024 * 1024, transcendentals=0
        ),
        name="partial",
    )(strain.transpose(1, 0, 2), table)


def whiten_kernel(x_ref, out_ref):
    rows, cols = x_ref.shape
    low = lax.broadcasted_iota(jnp.int32, (rows, 128), 1) < F
    for p in range(cols // 128):
        at = slice(p * 128, p * 128 + 128)
        spec = x_ref[:, at]
        square = spec * spec
        first = jnp.sum(jnp.where(low, square, 0.0), axis=1, keepdims=True)
        second = jnp.sum(jnp.where(low, 0.0, square), axis=1, keepdims=True)
        power = jnp.where(low, first, second) * (1.0 / F)
        out_ref[:, at] = (spec * lax.rsqrt(power + 1e-06 * SCALE * SCALE)).astype(out_ref.dtype)


def whiten(spectrum):
    return pl.pallas_call(
        whiten_kernel,
        out_shape=jax.ShapeDtypeStruct(spectrum.shape, jnp.bfloat16),
        compiler_params=pltpu.CompilerParams(vmem_limit_bytes=VMEM),
        name="whiten",
    )(spectrum)


def first_cross_kernel(blocks, own_ref, *rest):
    out_ref, stacked_ref, slots, sems = rest[-4:]
    rows, feats = own_ref.shape
    real = lax.broadcasted_iota(jnp.int32, (rows, 128), 1) % F < K
    stacked_ref[:rows] = own_ref[...]
    for k in range(feats // 128):
        at = slice(k * 128, k * 128 + 128)
        part = own_ref[:, at].astype(jnp.float32)
        turned = jnp.where(real, pltpu.roll(part, 128 - K, 1), -pltpu.roll(part, K, 1))
        stacked_ref[rows:, at] = turned.astype(stacked_ref.dtype)
    cross_kernel(blocks, stacked_ref, *rest[:-4], out_ref, slots, sems)


def cross_kernel(blocks, stacked_ref, *rest):
    out_ref, slots, sems = rest[-3:]
    rows = stacked_ref.shape[0] // 2
    n_y, n_zh = lax.axis_size("y"), lax.axis_size("zh")
    y, own_core = lax.axis_index("y"), lax.axis_index("core")
    copies = []
    for at, (operand, block, offset, zh, other) in enumerate(blocks):
        core = 1 - own_core if other else own_core
        column = ((y + offset) % n_y * n_zh + zh) * 2 + core
        columns = pl.ds(pl.multiple_of(column * rows, rows), rows)
        turned = rest[operand][block * rows : (block + 1) * rows].T
        for part in range(2):
            product = jnp.dot(stacked_ref[part * rows : (part + 1) * rows], turned, preferred_element_type=jnp.float32)
            slots[at, part] = (product * (1.0 / F)).astype(out_ref.dtype)
            copies.append(pltpu.make_async_copy(slots.at[at, part], out_ref.at[0, part, :, columns], sems.at[at, part]))
            copies[-1].start()
    for copy in copies:
        copy.wait()


def cross(stacked, pieces, total, partial):
    begin = partial is None
    rows, feats = stacked.shape[0] // (1 if begin else 2), stacked.shape[1]
    blocks, args = [], []
    for i, (piece, places) in enumerate(pieces):
        args.append(piece)
        blocks += [(i, j) + where for j, where in enumerate(places)]
    in_specs = [pl.BlockSpec(memory_space=pltpu.VMEM)] * (1 + len(args))
    out_specs = [pl.BlockSpec(memory_space=pl.ANY)]
    out_shape = [jax.ShapeDtypeStruct((1, 2, rows, total * rows), jnp.bfloat16)]
    aliases = {}
    if begin:
        out_specs.append(pl.BlockSpec(memory_space=pltpu.VMEM))
        out_shape.append(jax.ShapeDtypeStruct((2 * rows, feats), jnp.bfloat16))
    else:
        args.append(partial)
        in_specs.append(pl.BlockSpec(memory_space=pl.ANY))
        aliases = {len(args): 0}
    result = pl.pallas_call(
        functools.partial(first_cross_kernel if begin else cross_kernel, blocks),
        in_specs=in_specs,
        out_specs=out_specs,
        scratch_shapes=[
            pltpu.VMEM((len(blocks), 2, rows, rows), jnp.bfloat16),
            pltpu.SemaphoreType.DMA((len(blocks), 2)),
        ],
        out_shape=out_shape,
        input_output_aliases=aliases,
        compiler_params=pltpu.CompilerParams(vmem_limit_bytes=VMEM),
        cost_estimate=pl.CostEstimate(flops=len(blocks), bytes_accessed=len(blocks), transcendentals=0),
        name="cross",
    )(stacked, *args)
    return result if begin else result[0]


def shards(strain, band_start):
    n_y, n_zh = lax.axis_size("y"), lax.axis_size("zh")
    total = n_y * n_zh * lax.axis_size("core")

    def turn(piece, by):
        return lax.ppermute(piece, "y", [(i, (i + by) % n_y) for i in range(n_y)])

    def swap(piece):
        return lax.ppermute(piece, "core", [(0, 1), (1, 0)])

    sums = partial_spectra(strain, band_start).astype(jnp.float16)
    moved = lax.all_to_all(sums, BAND, 0, 0, tiled=True)
    own = whiten(jnp.sum(moved.astype(jnp.float32), axis=0))
    chans = own.shape[0]
    panel = lax.all_gather(own, "zh", axis=0, tiled=True)

    half = panel.shape[0] // 2
    zh_half = n_zh // 2
    top, bottom = panel[:half], panel[half:]
    back_top, ahead_bottom = turn(top, 1), turn(bottom, -1)
    far_top, far_bottom = turn(back_top, 1), turn(ahead_bottom, -1)
    swapped = swap(panel)

    def blocks(other):
        near_blocks = [(n_y - 1, z) for z in range(zh_half)] + [(1, z) for z in range(zh_half, n_zh)]
        near_blocks += [(n_y - 1, z) for z in range(zh_half, n_zh)] + [(1, z) for z in range(zh_half)]
        return (
            [(0, z, other) for z in range(n_zh)],
            [(offset, z, other) for offset, z in near_blocks],
            [(2, z, other) for z in range(n_zh)],
        )

    here, near_here, far_here = blocks(False)
    there, near_there, far_there = blocks(True)
    out, stacked = cross(own, [(panel, here)], total, None)
    top, bottom, out = lax.optimization_barrier((top, bottom, out))
    back_bottom, ahead_top = turn(bottom, 1), turn(top, -1)
    near = jnp.concatenate([back_top, ahead_bottom, back_bottom, ahead_top])
    out = cross(stacked, [(swapped, there), (near, near_here)], total, out)
    first, second, out = lax.optimization_barrier((near[: 2 * half], near[2 * half :], out))
    near_pieces = [(swap(first), near_there[:n_zh]), (swap(second), near_there[n_zh:])]
    far_top, far_bottom, out = lax.optimization_barrier((far_top, far_bottom, out))
    far_swapped = swap(jnp.concatenate([far_top, far_bottom]))
    pieces = near_pieces + [(far_top, far_here[:zh_half]), (far_bottom, far_here[zh_half:])]
    out = cross(stacked, pieces, total, out)
    return cross(stacked, [(far_swapped, far_there)], total, out)


def solution(mesh):
    parts = Mesh(mesh.devices.reshape(4, 4, 2, 4, 2), ("y", "zh", "core", "x", "zl"))
    return jax.shard_map(
        shards,
        mesh=parts,
        in_specs=(P(CHAN, None, BAND), P()),
        out_specs=P(BAND, None, CHAN, None),
        check_vma=False,
    )
```
